512 devices in a mesh: tm: 64 (over x, z), strip: 8 (over y, core).
Axes of the slice: x: 4, y: 4, z: 16, core: 2. Of those that a mesh axis runs over, the one named last changes fastest.
Arguments:
- frames: bfloat16 [2048, 128, 2048], P('tm', None, 'strip'), may hold values from -16 to 16
- freqs: int32 [16], replicated, may hold values from 1 to 64
- valid: int32 [128, 2048], P('tm', 'strip'), may hold values 0 or 1
- classes: int32 [128, 2048], P('tm', 'strip'), may hold values from 0 to 3
Outputs:
- smoothed: float32 [3, 128, 2048], P(None, 'tm', 'strip')
The draws below stay inside these ranges and needn't reach their ends.
All inputs are finite; a program needn't handle non-finite values. No bound on the sum of `valid` on one device may be relied on, other than what follows from the above.
Results may differ from the reference program's by a relative error of at most 0.00049.
Values may be sent and summed in bfloat16 or wider, within the bound.
No kernel may reach another device: no remote copies, remote signals or barrier semaphores. Data moves between devices by JAX's collectives and lax.ppermute only.
A program may use at most 64 MiB of HBM per device.

```python
import math
import jax
import jax.numpy as jnp
from jax import lax

H = 16
FR_DEV = 32
TV_PASSES = 3
FRAMES = 2048
ROWS = 128
COLS = 2048
N_TM = 64


def place_ends(values, key, smallest, top_value):
    index_at = [jax.random.randint(jax.random.fold_in(key, axis), (), 0, length) for axis, length in enumerate(values.shape)]
    main_axis = values.shape.index(max(values.shape))
    beside = index_at[:main_axis] + [(index_at[main_axis] + 1) % values.shape[main_axis]] + index_at[main_axis + 1:]
    return values.at[tuple(index_at)].set(smallest).at[tuple(beside)].set(top_value)


def raised(result, own_key, source, target, shards_of, factor):
    def block_of(dim):
        return (jnp.arange(result.shape[dim]) // (result.shape[dim] // shards_of)).reshape((-1,) + (1,) * (result.ndim - 1 - dim))

    first = jax.random.permutation(own_key, shards_of)[block_of(target)]
    far = (block_of(target) + shards_of // 2) % shards_of
    return jnp.where((block_of(source) == first) | (block_of(source) == far), factor * result, result)


def block_scale(key, shape, cuts, low, top_value):
    gain, own = 1.0, jax.random.fold_in(key, 6)
    for dim, parts in cuts:
        heights = jnp.exp(jax.random.uniform(jax.random.fold_in(own, dim), (parts,), jnp.float32, low / len(cuts), top_value / len(cuts)))
        gain = gain * jnp.repeat(heights, shape[dim] // parts).reshape([-1 if axis == dim else 1 for axis in range(len(shape))])
    return gain


def heavy_noise(own_key, dims, width, bound, split, heavy, kind=jnp.bfloat16):
    array = width * jax.random.normal(own_key, dims, jnp.float32)
    if split:
        array = array * block_scale(own_key, dims, split, -0.22, 0.18)
    return jnp.clip(raised(array, jax.random.fold_in(own_key, 3), *heavy), -bound, bound).astype(kind)


def setup_inputs(seed: int = 0) -> dict:
    streams_of = jax.random.split(jax.random.key(seed), 5)
    return {
        "frames": heavy_noise(streams_of[0], (FRAMES, ROWS, COLS), 1.0, 16.0, ((0, 64), (2, 8)), (0, 1, 64, 4.0)),
        "freqs": place_ends(jax.random.randint(streams_of[1], (H,), 1, 4 * H + 1), jax.random.fold_in(streams_of[1], 1), 1, 4 * H).astype(jnp.int32),
        "valid": place_ends((jax.random.randint(streams_of[2], (ROWS, COLS), 0, 4) < 3).astype(jnp.int32), jax.random.fold_in(streams_of[2], 1), 0, 1),
        "classes": place_ends(jax.random.randint(streams_of[3], (ROWS, COLS), 0, 4), jax.random.fold_in(streams_of[3], 1), 0, 3).astype(jnp.int32),
    }


EPS_TV = 1.0
STEP_TV = 0.2

def angle_table(freqs, times, total):
    phase = freqs[:, None] * times[None, :] % total
    angle = phase.astype(jnp.float32) * (2.0 * math.pi / total)
    return jnp.concatenate([jnp.cos(angle), -jnp.sin(angle)], axis=0).astype(jnp.bfloat16)

def start_params(classes):
    level = classes.astype(jnp.float32)
    return jnp.stack([-0.3 + 0.2 * level, 0.5 - 0.3 * level, -0.5 + 0.25 * level])

def gauss_newton(y_re, y_im, start, freqs, valid):
    alpha_par, beta_par, gamma_par = (start[0], start[1], start[2])
    weight = jnp.sqrt(freqs.astype(jnp.float32) / 8.0)[:, None, None]
    amp = jnp.exp(alpha_par)
    tanh_b = jnp.tanh(beta_par)
    refl = 0.8 * tanh_b
    slope = 0.8 * (1.0 - tanh_b * tanh_b)
    depth = jnp.exp(gamma_par) * weight
    decay = jnp.exp(-2.0 * depth)
    e_re = decay * jnp.cos(2.0 * depth)
    e_im = -decay * jnp.sin(2.0 * depth)
    g_re = refl * e_re
    g_im = refl * e_im
    d_re = 1.0 - g_re
    d_im = -g_im
    denom = d_re * d_re + d_im * d_im
    q_re = ((1.0 + g_re) * d_re + g_im * d_im) / denom
    q_im = (g_im * d_re - (1.0 + g_re) * d_im) / denom
    scale = amp / (math.sqrt(2.0) * weight)

    def project(z_re, z_im):
        return (scale * (z_re + z_im), scale * (z_im - z_re))
    m_re, m_im = project(q_re, q_im)
    den_sq = denom * denom
    p_re = 2.0 * (d_re * d_re - d_im * d_im) / den_sq
    p_im = -4.0 * d_re * d_im / den_sq
    zb_re = (p_re * e_re - p_im * e_im) * slope
    zb_im = (p_re * e_im + p_im * e_re) * slope
    h_re = -2.0 * depth * (g_re - g_im)
    h_im = -2.0 * depth * (g_re + g_im)
    zc_re = p_re * h_re - p_im * h_im
    zc_im = p_re * h_im + p_im * h_re
    columns = [(m_re, m_im), project(zb_re, zb_im), project(zc_re, zc_im)]
    res_re = y_re - m_re
    res_im = y_im - m_im
    mat = [[lax.optimization_barrier(jnp.sum(columns[i][0] * columns[j][0] + columns[i][1] * columns[j][1], axis=0)) for j in range(3)] for i in range(3)]
    rhs = [lax.optimization_barrier(jnp.sum(columns[i][0] * res_re + columns[i][1] * res_im, axis=0)) for i in range(3)]
    damping = 0.1 * (mat[0][0] + mat[1][1] + mat[2][2]) / 3.0 + 0.01
    a00 = mat[0][0] + damping
    a11 = mat[1][1] + damping
    a22 = mat[2][2] + damping
    a01 = mat[0][1]
    a02 = mat[0][2]
    a12 = mat[1][2]
    c00 = a11 * a22 - a12 * a12
    c01 = a02 * a12 - a01 * a22
    c02 = a01 * a12 - a02 * a11
    c11 = a00 * a22 - a02 * a02
    c12 = a01 * a02 - a00 * a12
    c22 = a00 * a11 - a01 * a01
    determinant = a00 * c00 + a01 * c01 + a02 * c02
    delta = jnp.stack([(c00 * rhs[0] + c01 * rhs[1] + c02 * rhs[2]) / determinant, (c01 * rhs[0] + c11 * rhs[1] + c12 * rhs[2]) / determinant, (c02 * rhs[0] + c12 * rhs[1] + c22 * rhs[2]) / determinant])
    return jnp.where(valid[None] == 1, start + delta, start)

def tv_pass(padded, field, fitted, row_first, col_first, rows_all, cols_all):
    rows_here = field.shape[1]
    cols_here = field.shape[2]
    grad_x = padded[:, 1:, :cols_here + 1] - padded[:, :rows_here + 1, :cols_here + 1]
    grad_y = padded[:, :rows_here + 1, 1:] - padded[:, :rows_here + 1, :cols_here + 1]
    row_ids = row_first - 1 + jnp.arange(rows_here + 1, dtype=jnp.int32)
    col_ids = col_first - 1 + jnp.arange(cols_here + 1, dtype=jnp.int32)
    row_good = (row_ids >= 0) & (row_ids <= rows_all - 2)
    col_good = (col_ids >= 0) & (col_ids <= cols_all - 2)
    grad_x = jnp.where(row_good[None, :, None], grad_x, jnp.float32(0.0))
    grad_y = jnp.where(col_good[None, None, :], grad_y, jnp.float32(0.0))
    length = jnp.sqrt(grad_x * grad_x + grad_y * grad_y + EPS_TV * EPS_TV)
    flux_x = grad_x / length
    flux_y = grad_y / length
    diverge = flux_x[:, 1:, 1:] - flux_x[:, :-1, 1:] + flux_y[:, 1:, 1:] - flux_y[:, 1:, :-1]
    return field + STEP_TV * (diverge - (field - fitted))

def reference(frames, freqs, valid, classes):
    table = angle_table(freqs, jnp.arange(FRAMES, dtype=jnp.int32), FRAMES)
    table_blocks = table.reshape(2 * H, N_TM, FR_DEV).transpose(1, 0, 2)
    frame_blocks = frames.reshape(N_TM, FR_DEV, ROWS * COLS)

    def accumulate(total, pieces):
        return (total + jnp.dot(pieces[0], pieces[1], preferred_element_type=jnp.float32), None)
    spectrum, _ = lax.scan(accumulate, jnp.zeros((2 * H, ROWS * COLS), jnp.float32), (table_blocks, frame_blocks))
    spectrum = spectrum.reshape(2 * H, ROWS, COLS) / math.sqrt(FRAMES)
    start = start_params(classes)
    fitted = gauss_newton(spectrum[:H], spectrum[H:], start, freqs, valid)
    field = fitted
    for step in range(TV_PASSES):
        padded = jnp.pad(field, ((0, 0), (1, 1), (1, 1)))
        field = tv_pass(padded, field, fitted, 0, 0, ROWS, COLS)
    return field
```

```python
import math

import jax
import jax.numpy as jnp
import numpy as np
from jax import lax
from jax.experimental import pallas as pl
from jax.experimental.pallas import tpu as pltpu
from jax.sharding import Mesh, PartitionSpec as P

TV_PASSES = 3
EPS_TV = 1.0
STEP_TV = 0.2
CLASSES = 4
TM = ("x", "z")


def angle_table(freqs, times, total):
    phase = freqs[:, None] * times[None, :] % total
    angle = phase.astype(jnp.float32) * (2.0 * math.pi / total)
    return jnp.concatenate([jnp.cos(angle), -jnp.sin(angle)], axis=0).astype(jnp.bfloat16)


def start_params(classes):
    level = classes.astype(jnp.float32)
    return jnp.stack([-0.3 + 0.2 * level, 0.5 - 0.3 * level, -0.5 + 0.25 * level])


def model_pieces(start, freqs):
    alpha_par, beta_par, gamma_par = (start[0], start[1], start[2])
    weight = jnp.sqrt(freqs.astype(jnp.float32) / 8.0)[:, None]
    amp = jnp.exp(alpha_par)
    tanh_b = jnp.tanh(beta_par)
    refl = 0.8 * tanh_b
    slope = 0.8 * (1.0 - tanh_b * tanh_b)
    depth = jnp.exp(gamma_par) * weight
    decay = jnp.exp(-2.0 * depth)
    e_re = decay * jnp.cos(2.0 * depth)
    e_im = -decay * jnp.sin(2.0 * depth)
    g_re = refl * e_re
    g_im = refl * e_im
    d_re = 1.0 - g_re
    d_im = -g_im
    denom = d_re * d_re + d_im * d_im
    q_re = ((1.0 + g_re) * d_re + g_im * d_im) / denom
    q_im = (g_im * d_re - (1.0 + g_re) * d_im) / denom
    scale = amp / (math.sqrt(2.0) * weight)

    def project(z_re, z_im):
        return jnp.concatenate([scale * (z_re + z_im), scale * (z_im - z_re)], axis=0)

    den_sq = denom * denom
    p_re = 2.0 * (d_re * d_re - d_im * d_im) / den_sq
    p_im = -4.0 * d_re * d_im / den_sq
    zb_re = (p_re * e_re - p_im * e_im) * slope
    zb_im = (p_re * e_im + p_im * e_re) * slope
    h_re = -2.0 * depth * (g_re - g_im)
    h_im = -2.0 * depth * (g_re + g_im)
    zc_re = p_re * h_re - p_im * h_im
    zc_im = p_re * h_im + p_im * h_re
    return jnp.stack([project(q_re, q_im), project(zb_re, zb_im), project(zc_re, zc_im)])


def class_system(freqs, total_frames):
    start = start_params(jnp.arange(CLASSES, dtype=jnp.int32))
    jac = model_pieces(start, freqs)
    mat = jnp.sum(jac[:, None] * jac[None, :], axis=2)
    damping = 0.1 * (mat[0, 0] + mat[1, 1] + mat[2, 2]) / 3.0 + 0.01
    a00 = mat[0, 0] + damping
    a11 = mat[1, 1] + damping
    a22 = mat[2, 2] + damping
    a01 = mat[0, 1]
    a02 = mat[0, 2]
    a12 = mat[1, 2]
    c00 = a11 * a22 - a12 * a12
    c01 = a02 * a12 - a01 * a22
    c02 = a01 * a12 - a02 * a11
    c11 = a00 * a22 - a02 * a02
    c12 = a01 * a02 - a00 * a12
    c22 = a00 * a11 - a01 * a01
    determinant = a00 * c00 + a01 * c01 + a02 * c02
    inverse = jnp.stack(
        [jnp.stack([c00, c01, c02]), jnp.stack([c01, c11, c12]), jnp.stack([c02, c12, c22])]
    ) / determinant
    model_rhs = mat[:, 0]
    offset = jnp.sum(inverse * model_rhs[None], axis=1)
    rows = jnp.sum(inverse[:, :, None, :] * jac[None], axis=1) / math.sqrt(total_frames)
    return start, offset, rows


def split_terms(value):
    terms = []
    for _ in range(3):
        term = lax.reduce_precision(value, 8, 7)
        terms.append(term.astype(jnp.bfloat16))
        value = value - term
    return jnp.concatenate(terms, axis=0)


def project_kernel(place_ref, weights_ref, frames_ref, *outs):
    group = 16
    count, _, cols = frames_ref.shape
    sums = weights_ref.shape[0]
    tall, wide = sums * group, count * group
    pick_row = lax.broadcasted_iota(jnp.int32, (tall, sums), 0) // group
    pick_col = lax.broadcasted_iota(jnp.int32, (tall, sums), 1)
    spread_rows = (pick_row == pick_col).astype(jnp.float32).astype(jnp.bfloat16)
    copy_row = lax.broadcasted_iota(jnp.int32, (count, wide), 0)
    copy_col = lax.broadcasted_iota(jnp.int32, (count, wide), 1) // group
    spread_cols = (copy_row == copy_col).astype(jnp.float32).astype(jnp.bfloat16)
    tall_by = jnp.dot(spread_rows, weights_ref[...], preferred_element_type=jnp.float32)
    full = jnp.dot(tall_by.astype(jnp.bfloat16), spread_cols, preferred_element_type=jnp.float32)
    same = (
        lax.broadcasted_iota(jnp.int32, (tall, wide), 0) % group
        == lax.broadcasted_iota(jnp.int32, (tall, wide), 1) % group
    )
    matrix = jnp.where(same, full, 0.0).astype(jnp.bfloat16)
    third = tall // 3
    parts = len(outs)
    for shift, out_ref in enumerate(outs):
        rows = out_ref.shape[1]
        first = lax.rem(place_ref[0] + shift, parts) * rows
        for step in range(rows // group):
            begin = pl.multiple_of(first + step * group, group)
            block = frames_ref[:, pl.ds(begin, group), :].reshape(wide, cols)
            got = jnp.dot(matrix, block, preferred_element_type=jnp.float32)
            total = (got[2 * third :] + got[third : 2 * third]) + got[:third]
            out_ref[:, step * group : (step + 1) * group, :] = total.reshape(sums // 3, group, cols)


def project(place, weights, frames, parts):
    count, rows, cols = frames.shape
    sums = weights.shape[0] // 3
    vmem = pl.BlockSpec(memory_space=pltpu.VMEM)
    out = jax.ShapeDtypeStruct((sums, rows // parts, cols), jnp.float32)
    return pl.pallas_call(
        project_kernel,
        out_shape=[out] * parts,
        in_specs=[pl.BlockSpec(memory_space=pltpu.SMEM), vmem, vmem],
        out_specs=[vmem] * parts,
        compiler_params=pltpu.CompilerParams(vmem_limit_bytes=32 * 1024 * 1024),
        cost_estimate=pl.CostEstimate(
            flops=2 * 16 * weights.shape[0] * count * rows * cols,
            bytes_accessed=2 * frames.size + 4 * sums * rows * cols,
            transcendentals=0,
        ),
    )(place, weights, frames)


def shifted(block, axis, count, by):
    pairs = [(i, i + by) for i in range(count) if 0 <= i + by < count]
    return lax.ppermute(block, axis, pairs)


def tv_pass(field, fitted, row_first, col_first, rows_all, cols_all):
    rows = field.shape[1] - 1
    cols = field.shape[2] - 1
    here = field[:, :rows, :cols]
    row_ids = row_first + lax.broadcasted_iota(jnp.int32, (1, rows, cols), 1)
    col_ids = col_first + lax.broadcasted_iota(jnp.int32, (1, rows, cols), 2)
    grad_x = field[:, 1:, :cols] - here
    grad_y = field[:, :rows, 1:] - here
    grad_x = jnp.where((row_ids >= 0) & (row_ids <= rows_all - 2), grad_x, 0.0)
    grad_y = jnp.where((col_ids >= 0) & (col_ids <= cols_all - 2), grad_y, 0.0)
    length = jnp.sqrt(grad_x * grad_x + grad_y * grad_y + EPS_TV * EPS_TV)
    flux_x = grad_x / length
    flux_y = grad_y / length
    diverge = flux_x[:, 1:, 1:] - flux_x[:, :-1, 1:] + flux_y[:, 1:, 1:] - flux_y[:, 1:, :-1]
    inner = field[:, 1:rows, 1:cols]
    return inner + STEP_TV * (diverge - (inner - fitted))


def on_device(frames, freqs, valid, classes):
    frame_count = frames.shape[0]
    x_devs = lax.axis_size("x")
    z_devs = lax.axis_size("z")
    time_devs = x_devs * z_devs
    strip_devs = lax.axis_size("strip")
    total_frames = frame_count * time_devs
    tile_rows, tile_cols = valid.shape
    x_here = lax.axis_index("x")
    tm_here = lax.axis_index(TM)

    classes_z = lax.all_to_all(
        jnp.broadcast_to(classes[None], (z_devs, tile_rows, tile_cols)), "z", 0, 0, tiled=True
    )

    start, offset, rows = class_system(freqs, total_frames)
    times_here = tm_here * frame_count + jnp.arange(frame_count, dtype=jnp.int32)
    table_here = angle_table(freqs, times_here, total_frames).astype(jnp.float32)
    by_class = jnp.transpose(rows, (2, 0, 1)).reshape(CLASSES * 3, -1)
    weights = jnp.sum(by_class[:, :, None] * table_here[None], axis=1)
    place = jnp.full((1,), x_here, jnp.int32)
    sums = project(place, split_terms(weights), frames, x_devs)

    total = sums[0]
    for shift in range(1, x_devs):
        pairs = [(i, (i + shift) % x_devs) for i in range(x_devs)]
        total = total + lax.ppermute(sums[shift], "x", pairs)
    total = total.reshape(CLASSES, 3, z_devs, tile_rows, tile_cols)
    own = jnp.zeros(total.shape[1:], jnp.float32)
    for level in range(CLASSES):
        own = jnp.where((classes_z == level)[None], total[level], own)
    own = jnp.transpose(own, (1, 0, 2, 3))
    own = lax.all_to_all(own, "z", 0, 0, tiled=True)
    delta = jnp.sum(own, axis=0)
    here = start_params(classes)
    base = jnp.zeros_like(here)
    for level in range(CLASSES):
        base = jnp.where((classes == level)[None], offset[:, level][:, None, None], base)
    fitted = jnp.where(valid[None] == 1, here + (delta - base), here)

    wide = TV_PASSES
    left = shifted(fitted[:, :, tile_cols - wide :], "strip", strip_devs, 1)
    right = shifted(fitted[:, :, :wide], "strip", strip_devs, -1)
    band = jnp.concatenate([left, fitted, right], axis=2)
    pieces = [
        shifted(band[:, 1:], TM, time_devs, 2),
        shifted(band, TM, time_devs, 1),
        band,
        shifted(band, TM, time_devs, -1),
        shifted(band[:, :1], TM, time_devs, -2),
    ]
    field = jnp.concatenate(pieces, axis=1)
    row_first = tm_here * tile_rows - wide
    col_first = lax.axis_index("strip") * tile_cols - wide
    rows_all = tile_rows * time_devs
    cols_all = tile_cols * strip_devs
    fit = field
    for step in range(TV_PASSES):
        fit = fit[:, 1:-1, 1:-1]
        field = tv_pass(field, fit, row_first + step, col_first + step, rows_all, cols_all)
    return field


def solution(mesh):
    strip_devs = mesh.shape["strip"]
    x_devs = 4
    grid = Mesh(mesh.devices.reshape(x_devs, -1, strip_devs), ("x", "z", "strip"))
    placed = (P(TM, None, "strip"), P(), P(TM, "strip"), P(TM, "strip"))
    return jax.shard_map(
        on_device, mesh=grid, in_specs=placed, out_specs=P(None, TM, "strip"), check_vma=False
    )
```

```python
import math

import jax
import jax.numpy as jnp
import numpy as np
from jax import lax
from jax.experimental import pallas as pl
from jax.experimental.pallas import tpu as pltpu
from jax.sharding import Mesh, PartitionSpec as P

TV_PASSES = 3
EPS_TV = 1.0
STEP_TV = 0.2
CLASSES = 4
TM = ("x", "z")


def angle_table(freqs, times, total):
    phase = freqs[:, None] * times[None, :] % total
    angle = phase.astype(jnp.float32) * (2.0 * math.pi / total)
    return jnp.concatenate([jnp.cos(angle), -jnp.sin(angle)], axis=0).astype(jnp.bfloat16)


def start_params(classes):
    level = classes.astype(jnp.float32)
    return jnp.stack([-0.3 + 0.2 * level, 0.5 - 0.3 * level, -0.5 + 0.25 * level])


def model_pieces(start, freqs):
    alpha_par, beta_par, gamma_par = (start[0], start[1], start[2])
    weight = jnp.sqrt(freqs.astype(jnp.float32) / 8.0)[:, None]
    amp = jnp.exp(alpha_par)
    tanh_b = jnp.tanh(beta_par)
    refl = 0.8 * tanh_b
    slope = 0.8 * (1.0 - tanh_b * tanh_b)
    depth = jnp.exp(gamma_par) * weight
    decay = jnp.exp(-2.0 * depth)
    e_re = decay * jnp.cos(2.0 * depth)
    e_im = -decay * jnp.sin(2.0 * depth)
    g_re = refl * e_re
    g_im = refl * e_im
    d_re = 1.0 - g_re
    d_im = -g_im
    denom = d_re * d_re + d_im * d_im
    q_re = ((1.0 + g_re) * d_re + g_im * d_im) / denom
    q_im = (g_im * d_re - (1.0 + g_re) * d_im) / denom
    scale = amp / (math.sqrt(2.0) * weight)

    def project(z_re, z_im):
        return jnp.concatenate([scale * (z_re + z_im), scale * (z_im - z_re)], axis=0)

    den_sq = denom * denom
    p_re = 2.0 * (d_re * d_re - d_im * d_im) / den_sq
    p_im = -4.0 * d_re * d_im / den_sq
    zb_re = (p_re * e_re - p_im * e_im) * slope
    zb_im = (p_re * e_im + p_im * e_re) * slope
    h_re = -2.0 * depth * (g_re - g_im)
    h_im = -2.0 * depth * (g_re + g_im)
    zc_re = p_re * h_re - p_im * h_im
    zc_im = p_re * h_im + p_im * h_re
    return jnp.stack([project(q_re, q_im), project(zb_re, zb_im), project(zc_re, zc_im)])


def class_system(freqs, total_frames):
    start = start_params(jnp.arange(CLASSES, dtype=jnp.int32))
    jac = model_pieces(start, freqs)
    mat = jnp.sum(jac[:, None] * jac[None, :], axis=2)
    damping = 0.1 * (mat[0, 0] + mat[1, 1] + mat[2, 2]) / 3.0 + 0.01
    a00 = mat[0, 0] + damping
    a11 = mat[1, 1] + damping
    a22 = mat[2, 2] + damping
    a01 = mat[0, 1]
    a02 = mat[0, 2]
    a12 = mat[1, 2]
    c00 = a11 * a22 - a12 * a12
    c01 = a02 * a12 - a01 * a22
    c02 = a01 * a12 - a02 * a11
    c11 = a00 * a22 - a02 * a02
    c12 = a01 * a02 - a00 * a12
    c22 = a00 * a11 - a01 * a01
    determinant = a00 * c00 + a01 * c01 + a02 * c02
    inverse = jnp.stack(
        [jnp.stack([c00, c01, c02]), jnp.stack([c01, c11, c12]), jnp.stack([c02, c12, c22])]
    ) / determinant
    model_rhs = mat[:, 0]
    offset = jnp.sum(inverse * model_rhs[None], axis=1)
    rows = jnp.sum(inverse[:, :, None, :] * jac[None], axis=1) / math.sqrt(total_frames)
    return start, offset, rows


def split_terms(value):
    terms = []
    for _ in range(3):
        term = lax.reduce_precision(value, 8, 7)
        terms.append(term.astype(jnp.bfloat16))
        value = value - term
    return jnp.concatenate(terms, axis=0)


def project_kernel(place_ref, weights_ref, frames_ref, *outs):
    group = 16
    count, _, cols = frames_ref.shape
    sums = weights_ref.shape[0]
    tall, wide = sums * group, count * group
    pick_row = lax.broadcasted_iota(jnp.int32, (tall, sums), 0) // group
    pick_col = lax.broadcasted_iota(jnp.int32, (tall, sums), 1)
    spread_rows = (pick_row == pick_col).astype(jnp.float32).astype(jnp.bfloat16)
    copy_row = lax.broadcasted_iota(jnp.int32, (count, wide), 0)
    copy_col = lax.broadcasted_iota(jnp.int32, (count, wide), 1) // group
    spread_cols = (copy_row == copy_col).astype(jnp.float32).astype(jnp.bfloat16)
    tall_by = jnp.dot(spread_rows, weights_ref[...], preferred_element_type=jnp.float32)
    full = jnp.dot(tall_by.astype(jnp.bfloat16), spread_cols, preferred_element_type=jnp.float32)
    same = (
        lax.broadcasted_iota(jnp.int32, (tall, wide), 0) % group
        == lax.broadcasted_iota(jnp.int32, (tall, wide), 1) % group
    )
    matrix = jnp.where(same, full, 0.0).astype(jnp.bfloat16)
    third = tall // 3
    parts = len(outs)
    for shift, out_ref in enumerate(outs):
        rows = out_ref.shape[1]
        first = lax.rem(place_ref[0] + shift, parts) * rows
        for step in range(rows // group):
            begin = pl.multiple_of(first + step * group, group)
            block = frames_ref[:, pl.ds(begin, group), :].reshape(wide, cols)
            got = jnp.dot(matrix, block, preferred_element_type=jnp.float32)
            total = (got[2 * third :] + got[third : 2 * third]) + got[:third]
            out_ref[:, step * group : (step + 1) * group, :] = total.reshape(sums // 3, group, cols)


def project(place, weights, frames, parts):
    count, rows, cols = frames.shape
    sums = weights.shape[0] // 3
    vmem = pl.BlockSpec(memory_space=pltpu.VMEM)
    out = jax.ShapeDtypeStruct((sums, rows // parts, cols), jnp.float32)
    return pl.pallas_call(
        project_kernel,
        out_shape=[out] * parts,
        in_specs=[pl.BlockSpec(memory_space=pltpu.SMEM), vmem, vmem],
        out_specs=[vmem] * parts,
        compiler_params=pltpu.CompilerParams(vmem_limit_bytes=32 * 1024 * 1024),
        cost_estimate=pl.CostEstimate(
            flops=2 * 16 * weights.shape[0] * count * rows * cols,
            bytes_accessed=2 * frames.size + 4 * sums * rows * cols,
            transcendentals=0,
        ),
    )(place, weights, frames)


def exchange(block, count):
    middle = count // 2
    order = [(middle + i) % count for i in range(count)]
    block = jnp.concatenate([block[middle:], block[:middle]])
    got = lax.all_to_all(block, "z", 0, 0, axis_index_groups=[order], tiled=True)
    return jnp.concatenate([got[count - middle :], got[: count - middle]])


def shifted(block, axis, count, by):
    pairs = [(i, i + by) for i in range(count) if 0 <= i + by < count]
    return lax.ppermute(block, axis, pairs)


def tv_pass(field, fitted, row_first, col_first, rows_all, cols_all):
    rows = field.shape[1] - 1
    cols = field.shape[2] - 1
    here = field[:, :rows, :cols]
    row_ids = row_first + lax.broadcasted_iota(jnp.int32, (1, rows, cols), 1)
    col_ids = col_first + lax.broadcasted_iota(jnp.int32, (1, rows, cols), 2)
    grad_x = field[:, 1:, :cols] - here
    grad_y = field[:, :rows, 1:] - here
    grad_x = jnp.where((row_ids >= 0) & (row_ids <= rows_all - 2), grad_x, 0.0)
    grad_y = jnp.where((col_ids >= 0) & (col_ids <= cols_all - 2), grad_y, 0.0)
    length = jnp.sqrt(grad_x * grad_x + grad_y * grad_y + EPS_TV * EPS_TV)
    flux_x = grad_x / length
    flux_y = grad_y / length
    diverge = flux_x[:, 1:, 1:] - flux_x[:, :-1, 1:] + flux_y[:, 1:, 1:] - flux_y[:, 1:, :-1]
    inner = field[:, 1:rows, 1:cols]
    return inner + STEP_TV * (diverge - (inner - fitted))


def on_device(frames, freqs, valid, classes):
    frame_count = frames.shape[0]
    x_devs = lax.axis_size("x")
    z_devs = lax.axis_size("z")
    time_devs = x_devs * z_devs
    strip_devs = lax.axis_size("strip")
    total_frames = frame_count * time_devs
    tile_rows, tile_cols = valid.shape
    x_here = lax.axis_index("x")
    tm_here = lax.axis_index(TM)

    codes = classes + CLASSES * valid
    classes_z = exchange(jnp.broadcast_to(codes[None], (z_devs, *codes.shape)), z_devs)

    start, offset, rows = class_system(freqs, total_frames)
    times_here = tm_here * frame_count + jnp.arange(frame_count, dtype=jnp.int32)
    table_here = angle_table(freqs, times_here, total_frames).astype(jnp.float32)
    by_class = jnp.transpose(rows, (2, 0, 1)).reshape(CLASSES * 3, -1)
    weights = jnp.sum(by_class[:, :, None] * table_here[None], axis=1)
    place = jnp.full((1,), x_here, jnp.int32)
    sums = project(place, split_terms(weights), frames, x_devs)

    total = sums[0]
    for shift in range(1, x_devs):
        pairs = [(i, (i + shift) % x_devs) for i in range(x_devs)]
        total = total + lax.ppermute(sums[shift], "x", pairs)
    pair = 2 * tile_rows
    total = total.reshape(CLASSES, 3, z_devs // 2, pair, tile_cols)
    levels = classes_z.reshape(z_devs // 2, pair, tile_cols) % CLASSES
    own = jnp.zeros(total.shape[1:], jnp.float32)
    for level in range(CLASSES):
        own = jnp.where((levels == level)[None], total[level], own)
    own = jnp.transpose(own, (1, 0, 2, 3))
    own = jnp.broadcast_to(own[:, None], (z_devs // 2, 2, *own.shape[1:]))
    own = own.reshape(z_devs, 3, pair, tile_cols)
    own = exchange(own, z_devs)
    delta = jnp.sum(own, axis=0)
    codes = lax.dynamic_index_in_dim(
        classes_z.reshape(z_devs // 2, pair, tile_cols), lax.axis_index("z") // 2, 0, False
    )
    classes = codes % CLASSES
    here = start_params(classes)
    base = jnp.zeros_like(here)
    for level in range(CLASSES):
        base = jnp.where((classes == level)[None], offset[:, level][:, None, None], base)
    fitted = jnp.where((codes >= CLASSES)[None], here + (delta - base), here)

    wide = TV_PASSES
    left = shifted(fitted[:, :, tile_cols - wide :], "strip", strip_devs, 1)
    right = shifted(fitted[:, :, :wide], "strip", strip_devs, -1)
    band = jnp.concatenate([left, fitted, right], axis=2)
    above = shifted(band[:, pair - wide :], TM, time_devs, 2)
    below = shifted(band[:, :wide], TM, time_devs, -2)
    field = jnp.concatenate([above, band, below], axis=1)
    pair_first = lax.div(tm_here, 2) * pair
    row_first = pair_first - wide
    col_first = lax.axis_index("strip") * tile_cols - wide
    rows_all = tile_rows * time_devs
    cols_all = tile_cols * strip_devs
    fit = field
    for step in range(TV_PASSES):
        fit = fit[:, 1:-1, 1:-1]
        field = tv_pass(field, fit, row_first + step, col_first + step, rows_all, cols_all)
    return lax.dynamic_slice_in_dim(field, tm_here * tile_rows - pair_first, tile_rows, 1)


def solution(mesh):
    strip_devs = mesh.shape["strip"]
    x_devs = 4
    grid = Mesh(mesh.devices.reshape(x_devs, -1, strip_devs), ("x", "z", "strip"))
    placed = (P(TM, None, "strip"), P(), P(TM, "strip"), P(TM, "strip"))
    return jax.shard_map(
        on_device, mesh=grid, in_specs=placed, out_specs=P(None, TM, "strip"), check_vma=False
    )
```

```python
import math

import jax
import jax.numpy as jnp
import numpy as np
from jax import lax
from jax.experimental import pallas as pl
from jax.experimental.pallas import tpu as pltpu
from jax.sharding import Mesh, PartitionSpec as P

TV_PASSES = 3
EPS_TV = 1.0
STEP_TV = 0.2
CLASSES = 4
TM = ("x", "z")
FIRST_Z = 12


def angle_table(freqs, times, total):
    phase = freqs[:, None] * times[None, :] % total
    angle = phase.astype(jnp.float32) * (2.0 * math.pi / total)
    return jnp.concatenate([jnp.cos(angle), -jnp.sin(angle)], axis=0).astype(jnp.bfloat16)


def start_params(classes):
    level = classes.astype(jnp.float32)
    return jnp.stack([-0.3 + 0.2 * level, 0.5 - 0.3 * level, -0.5 + 0.25 * level])


def model_pieces(start, freqs):
    alpha_par, beta_par, gamma_par = (start[0], start[1], start[2])
    weight = jnp.sqrt(freqs.astype(jnp.float32) / 8.0)[:, None]
    amp = jnp.exp(alpha_par)
    tanh_b = jnp.tanh(beta_par)
    refl = 0.8 * tanh_b
    slope = 0.8 * (1.0 - tanh_b * tanh_b)
    depth = jnp.exp(gamma_par) * weight
    decay = jnp.exp(-2.0 * depth)
    e_re = decay * jnp.cos(2.0 * depth)
    e_im = -decay * jnp.sin(2.0 * depth)
    g_re = refl * e_re
    g_im = refl * e_im
    d_re = 1.0 - g_re
    d_im = -g_im
    denom = d_re * d_re + d_im * d_im
    q_re = ((1.0 + g_re) * d_re + g_im * d_im) / denom
    q_im = (g_im * d_re - (1.0 + g_re) * d_im) / denom
    scale = amp / (math.sqrt(2.0) * weight)

    def project(z_re, z_im):
        return jnp.concatenate([scale * (z_re + z_im), scale * (z_im - z_re)], axis=0)

    den_sq = denom * denom
    p_re = 2.0 * (d_re * d_re - d_im * d_im) / den_sq
    p_im = -4.0 * d_re * d_im / den_sq
    zb_re = (p_re * e_re - p_im * e_im) * slope
    zb_im = (p_re * e_im + p_im * e_re) * slope
    h_re = -2.0 * depth * (g_re - g_im)
    h_im = -2.0 * depth * (g_re + g_im)
    zc_re = p_re * h_re - p_im * h_im
    zc_im = p_re * h_im + p_im * h_re
    return jnp.stack([project(q_re, q_im), project(zb_re, zb_im), project(zc_re, zc_im)])


def class_system(freqs, total_frames):
    start = start_params(jnp.arange(CLASSES, dtype=jnp.int32))
    jac = model_pieces(start, freqs)
    mat = jnp.sum(jac[:, None] * jac[None, :], axis=2)
    damping = 0.1 * (mat[0, 0] + mat[1, 1] + mat[2, 2]) / 3.0 + 0.01
    a00 = mat[0, 0] + damping
    a11 = mat[1, 1] + damping
    a22 = mat[2, 2] + damping
    a01 = mat[0, 1]
    a02 = mat[0, 2]
    a12 = mat[1, 2]
    c00 = a11 * a22 - a12 * a12
    c01 = a02 * a12 - a01 * a22
    c02 = a01 * a12 - a02 * a11
    c11 = a00 * a22 - a02 * a02
    c12 = a01 * a02 - a00 * a12
    c22 = a00 * a11 - a01 * a01
    determinant = a00 * c00 + a01 * c01 + a02 * c02
    inverse = jnp.stack(
        [jnp.stack([c00, c01, c02]), jnp.stack([c01, c11, c12]), jnp.stack([c02, c12, c22])]
    ) / determinant
    model_rhs = mat[:, 0]
    offset = jnp.sum(inverse * model_rhs[None], axis=1)
    rows = jnp.sum(inverse[:, :, None, :] * jac[None], axis=1) / math.sqrt(total_frames)
    return start, offset, rows


def split_terms(value):
    terms = []
    for _ in range(3):
        term = lax.reduce_precision(value, 8, 7)
        terms.append(term.astype(jnp.bfloat16))
        value = value - term
    return jnp.concatenate(terms, axis=0)


def project_kernel(place_ref, weights_ref, frames_ref, *outs):
    group = 16
    count, _, cols = frames_ref.shape
    sums = weights_ref.shape[0]
    tall, wide = sums * group, count * group
    pick_row = lax.broadcasted_iota(jnp.int32, (tall, sums), 0) // group
    pick_col = lax.broadcasted_iota(jnp.int32, (tall, sums), 1)
    spread_rows = (pick_row == pick_col).astype(jnp.float32).astype(jnp.bfloat16)
    copy_row = lax.broadcasted_iota(jnp.int32, (count, wide), 0)
    copy_col = lax.broadcasted_iota(jnp.int32, (count, wide), 1) // group
    spread_cols = (copy_row == copy_col).astype(jnp.float32).astype(jnp.bfloat16)
    tall_by = jnp.dot(spread_rows, weights_ref[...], preferred_element_type=jnp.float32)
    full = jnp.dot(tall_by.astype(jnp.bfloat16), spread_cols, preferred_element_type=jnp.float32)
    same = (
        lax.broadcasted_iota(jnp.int32, (tall, wide), 0) % group
        == lax.broadcasted_iota(jnp.int32, (tall, wide), 1) % group
    )
    matrix = jnp.where(same, full, 0.0).astype(jnp.bfloat16)
    third = tall // 3
    parts = len(outs)
    for shift, out_ref in enumerate(outs):
        rows = out_ref.shape[1]
        first = lax.rem(place_ref[0] + shift, parts) * rows
        for step in range(rows // group):
            begin = pl.multiple_of(first + step * group, group)
            block = frames_ref[:, pl.ds(begin, group), :].reshape(wide, cols)
            got = jnp.dot(matrix, block, preferred_element_type=jnp.float32)
            total = (got[2 * third :] + got[third : 2 * third]) + got[:third]
            out_ref[:, step * group : (step + 1) * group, :] = total.reshape(sums // 3, group, cols)


def project(place, weights, frames, parts):
    count, rows, cols = frames.shape
    sums = weights.shape[0] // 3
    vmem = pl.BlockSpec(memory_space=pltpu.VMEM)
    out = jax.ShapeDtypeStruct((sums, rows // parts, cols), jnp.float32)
    return pl.pallas_call(
        project_kernel,
        out_shape=[out] * parts,
        in_specs=[pl.BlockSpec(memory_space=pltpu.SMEM), vmem, vmem],
        out_specs=[vmem] * parts,
        compiler_params=pltpu.CompilerParams(vmem_limit_bytes=32 * 1024 * 1024),
        cost_estimate=pl.CostEstimate(
            flops=2 * 16 * weights.shape[0] * count * rows * cols,
            bytes_accessed=2 * frames.size + 4 * sums * rows * cols,
            transcendentals=0,
        ),
    )(place, weights, frames)


def choose_kernel(codes_ref, *refs):
    *sums_refs, out_ref = refs
    kinds, rows, cols = sums_refs[0].shape
    half = cols // 2
    params = kinds // CLASSES
    targets, planes, pair, _ = out_ref.shape
    shown = targets * pair // rows
    for plane in range(planes):
        first = plane // params * half
        level = codes_ref[:, first : first + half] & (CLASSES - 1)
        own = None
        for kind in range(CLASSES):
            at = (kind * params + plane % params, slice(None), slice(first, first + half))
            total = (sums_refs[0][at] + sums_refs[1][at]) + (sums_refs[2][at] + sums_refs[3][at])
            own = total if own is None else jnp.where(level == kind, total, own)
        for target in range(targets):
            begin = (target + FIRST_Z) % targets // shown * pair
            out_ref[target, plane] = own[begin : begin + pair]


def choose(codes, sums, targets, pair):
    kinds, _, cols = sums[0].shape
    vmem = pl.BlockSpec(memory_space=pltpu.VMEM)
    planes = 2 * (kinds // CLASSES)
    return pl.pallas_call(
        choose_kernel,
        out_shape=jax.ShapeDtypeStruct((targets, planes, pair, cols // 2), jnp.float32),
        in_specs=[vmem] * (1 + len(sums)),
        out_specs=vmem,
        compiler_params=pltpu.CompilerParams(vmem_limit_bytes=32 * 1024 * 1024),
    )(codes, *sums)


def exchange(block, count):
    order = [(FIRST_Z + i) % count for i in range(count)]
    return lax.all_to_all(block, "z", 0, 0, axis_index_groups=[order], tiled=True)


def shifted(block, axis, count, by):
    pairs = [(i, i + by) for i in range(count) if 0 <= i + by < count]
    return lax.ppermute(block, axis, pairs)


def tv_pass(field, fitted, row_first, col_first, rows_all, cols_all):
    rows = field.shape[1] - 1
    cols = field.shape[2] - 1
    here = field[:, :rows, :cols]
    row_ids = row_first + lax.broadcasted_iota(jnp.int32, (1, rows, cols), 1)
    col_ids = col_first + lax.broadcasted_iota(jnp.int32, (1, rows, cols), 2)
    grad_x = field[:, 1:, :cols] - here
    grad_y = field[:, :rows, 1:] - here
    grad_x = jnp.where((row_ids >= 0) & (row_ids <= rows_all - 2), grad_x, 0.0)
    grad_y = jnp.where((col_ids >= 0) & (col_ids <= cols_all - 2), grad_y, 0.0)
    length = jnp.sqrt(grad_x * grad_x + grad_y * grad_y + EPS_TV * EPS_TV)
    flux_x = grad_x / length
    flux_y = grad_y / length
    diverge = flux_x[:, 1:, 1:] - flux_x[:, :-1, 1:] + flux_y[:, 1:, 1:] - flux_y[:, 1:, :-1]
    inner = field[:, 1:rows, 1:cols]
    return inner + STEP_TV * (diverge - (inner - fitted))


def on_device(frames, freqs, valid, classes):
    frame_count = frames.shape[0]
    x_devs = lax.axis_size("x")
    z_devs = lax.axis_size("z")
    time_devs = x_devs * z_devs
    strip_devs = lax.axis_size("strip")
    total_frames = frame_count * time_devs
    tile_rows, tile_cols = valid.shape
    x_here = lax.axis_index("x")
    tm_here = lax.axis_index(TM)

    pair = 2 * tile_rows
    codes = classes + CLASSES * valid
    codes = exchange(jnp.broadcast_to(codes[None], (z_devs, *codes.shape)), z_devs)
    codes = jnp.concatenate([codes[z_devs - FIRST_Z :], codes[: z_devs - FIRST_Z]])
    codes = codes.reshape(-1, tile_cols)

    start, offset, rows = class_system(freqs, total_frames)
    times_here = tm_here * frame_count + jnp.arange(frame_count, dtype=jnp.int32)
    table_here = angle_table(freqs, times_here, total_frames).astype(jnp.float32)
    by_class = jnp.transpose(rows, (2, 0, 1)).reshape(CLASSES * 3, -1)
    weights = jnp.sum(by_class[:, :, None] * table_here[None], axis=1)
    place = jnp.full((1,), x_here, jnp.int32)
    sums = project(place, split_terms(weights), frames, x_devs)

    parts = [sums[0]]
    for shift in range(1, x_devs):
        pairs = [(i, (i + shift) % x_devs) for i in range(x_devs)]
        parts.append(lax.ppermute(sums[shift], "x", pairs))
    own = choose(codes, parts, z_devs, pair)
    own = jnp.sum(exchange(own, z_devs), axis=0)
    delta = jnp.concatenate([own[:3], own[3:]], axis=2)
    codes = lax.dynamic_slice_in_dim(codes, lax.axis_index("z") // 2 * pair, pair, 0)
    classes = codes % CLASSES
    here = start_params(classes)
    base = jnp.zeros_like(here)
    for level in range(CLASSES):
        base = jnp.where((classes == level)[None], offset[:, level][:, None, None], base)
    fitted = jnp.where((codes >= CLASSES)[None], here + (delta - base), here)

    wide = TV_PASSES
    left = shifted(fitted[:, :, tile_cols - wide :], "strip", strip_devs, 1)
    right = shifted(fitted[:, :, :wide], "strip", strip_devs, -1)
    band = jnp.concatenate([left, fitted, right], axis=2)
    above = shifted(band[:, pair - wide :], TM, time_devs, 2)
    below = shifted(band[:, :wide], TM, time_devs, -2)
    field = jnp.concatenate([above, band, below], axis=1)
    pair_first = lax.div(tm_here, 2) * pair
    row_first = pair_first - wide
    col_first = lax.axis_index("strip") * tile_cols - wide
    rows_all = tile_rows * time_devs
    cols_all = tile_cols * strip_devs
    fit = field
    for step in range(TV_PASSES):
        fit = fit[:, 1:-1, 1:-1]
        field = tv_pass(field, fit, row_first + step, col_first + step, rows_all, cols_all)
    return lax.dynamic_slice_in_dim(field, tm_here * tile_rows - pair_first, tile_rows, 1)


def solution(mesh):
    strip_devs = mesh.shape["strip"]
    x_devs = 4
    grid = Mesh(mesh.devices.reshape(x_devs, -1, strip_devs), ("x", "z", "strip"))
    placed = (P(TM, None, "strip"), P(), P(TM, "strip"), P(TM, "strip"))
    return jax.shard_map(
        on_device, mesh=grid, in_specs=placed, out_specs=P(None, TM, "strip"), check_vma=False
    )
```

```python
import math

import jax
import jax.numpy as jnp
import numpy as np
from jax import lax
from jax.experimental import pallas as pl
from jax.experimental.pallas import tpu as pltpu
from jax.sharding import Mesh, PartitionSpec as P

TV_PASSES = 3
EPS_TV = 1.0
STEP_TV = 0.2
CLASSES = 4
TM = ("x", "z")
FIRST_Z = 11


def angle_table(freqs, times, total):
    phase = freqs[:, None] * times[None, :] % total
    angle = phase.astype(jnp.float32) * (2.0 * math.pi / total)
    return jnp.concatenate([jnp.cos(angle), -jnp.sin(angle)], axis=0).astype(jnp.bfloat16)


def start_params(classes):
    level = classes.astype(jnp.float32)
    return jnp.stack([-0.3 + 0.2 * level, 0.5 - 0.3 * level, -0.5 + 0.25 * level])


def model_pieces(start, freqs):
    alpha_par, beta_par, gamma_par = (start[0], start[1], start[2])
    weight = jnp.sqrt(freqs.astype(jnp.float32) / 8.0)[:, None]
    amp = jnp.exp(alpha_par)
    tanh_b = jnp.tanh(beta_par)
    refl = 0.8 * tanh_b
    slope = 0.8 * (1.0 - tanh_b * tanh_b)
    depth = jnp.exp(gamma_par) * weight
    decay = jnp.exp(-2.0 * depth)
    e_re = decay * jnp.cos(2.0 * depth)
    e_im = -decay * jnp.sin(2.0 * depth)
    g_re = refl * e_re
    g_im = refl * e_im
    d_re = 1.0 - g_re
    d_im = -g_im
    denom = d_re * d_re + d_im * d_im
    q_re = ((1.0 + g_re) * d_re + g_im * d_im) / denom
    q_im = (g_im * d_re - (1.0 + g_re) * d_im) / denom
    scale = amp / (math.sqrt(2.0) * weight)

    def project(z_re, z_im):
        return jnp.concatenate([scale * (z_re + z_im), scale * (z_im - z_re)], axis=0)

    den_sq = denom * denom
    p_re = 2.0 * (d_re * d_re - d_im * d_im) / den_sq
    p_im = -4.0 * d_re * d_im / den_sq
    zb_re = (p_re * e_re - p_im * e_im) * slope
    zb_im = (p_re * e_im + p_im * e_re) * slope
    h_re = -2.0 * depth * (g_re - g_im)
    h_im = -2.0 * depth * (g_re + g_im)
    zc_re = p_re * h_re - p_im * h_im
    zc_im = p_re * h_im + p_im * h_re
    return jnp.stack([project(q_re, q_im), project(zb_re, zb_im), project(zc_re, zc_im)])


def class_system(freqs, total_frames):
    start = start_params(jnp.arange(CLASSES, dtype=jnp.int32))
    jac = model_pieces(start, freqs)
    mat = jnp.sum(jac[:, None] * jac[None, :], axis=2)
    damping = 0.1 * (mat[0, 0] + mat[1, 1] + mat[2, 2]) / 3.0 + 0.01
    a00 = mat[0, 0] + damping
    a11 = mat[1, 1] + damping
    a22 = mat[2, 2] + damping
    a01 = mat[0, 1]
    a02 = mat[0, 2]
    a12 = mat[1, 2]
    c00 = a11 * a22 - a12 * a12
    c01 = a02 * a12 - a01 * a22
    c02 = a01 * a12 - a02 * a11
    c11 = a00 * a22 - a02 * a02
    c12 = a01 * a02 - a00 * a12
    c22 = a00 * a11 - a01 * a01
    determinant = a00 * c00 + a01 * c01 + a02 * c02
    inverse = jnp.stack(
        [jnp.stack([c00, c01, c02]), jnp.stack([c01, c11, c12]), jnp.stack([c02, c12, c22])]
    ) / determinant
    model_rhs = mat[:, 0]
    offset = jnp.sum(inverse * model_rhs[None], axis=1)
    rows = jnp.sum(inverse[:, :, None, :] * jac[None], axis=1) / math.sqrt(total_frames)
    return start, offset, rows


def split_terms(value):
    terms = []
    for _ in range(3):
        term = lax.reduce_precision(value, 8, 7)
        terms.append(term.astype(jnp.bfloat16))
        value = value - term
    return jnp.concatenate(terms, axis=0)


def project_kernel(place_ref, weights_ref, frames_ref, *outs):
    group = 16
    count, _, cols = frames_ref.shape
    sums = weights_ref.shape[0]
    tall, wide = sums * group, count * group
    pick_row = lax.broadcasted_iota(jnp.int32, (tall, sums), 0) // group
    pick_col = lax.broadcasted_iota(jnp.int32, (tall, sums), 1)
    spread_rows = (pick_row == pick_col).astype(jnp.float32).astype(jnp.bfloat16)
    copy_row = lax.broadcasted_iota(jnp.int32, (count, wide), 0)
    copy_col = lax.broadcasted_iota(jnp.int32, (count, wide), 1) // group
    spread_cols = (copy_row == copy_col).astype(jnp.float32).astype(jnp.bfloat16)
    tall_by = jnp.dot(spread_rows, weights_ref[...], preferred_element_type=jnp.float32)
    full = jnp.dot(tall_by.astype(jnp.bfloat16), spread_cols, preferred_element_type=jnp.float32)
    same = (
        lax.broadcasted_iota(jnp.int32, (tall, wide), 0) % group
        == lax.broadcasted_iota(jnp.int32, (tall, wide), 1) % group
    )
    matrix = jnp.where(same, full, 0.0).astype(jnp.bfloat16)
    third = tall // 3
    parts = len(outs)
    for shift, out_ref in enumerate(outs):
        rows = out_ref.shape[1]
        first = lax.rem(place_ref[0] + shift, parts) * rows
        for step in range(rows // group):
            begin = pl.multiple_of(first + step * group, group)
            block = frames_ref[:, pl.ds(begin, group), :].reshape(wide, cols)
            got = jnp.dot(matrix, block, preferred_element_type=jnp.float32)
            total = (got[2 * third :] + got[third : 2 * third]) + got[:third]
            out_ref[:, step * group : (step + 1) * group, :] = total.reshape(sums // 3, group, cols)


def project(place, weights, frames, parts):
    count, rows, cols = frames.shape
    sums = weights.shape[0] // 3
    vmem = pl.BlockSpec(memory_space=pltpu.VMEM)
    out = jax.ShapeDtypeStruct((sums, rows // parts, cols), jnp.float32)
    return pl.pallas_call(
        project_kernel,
        out_shape=[out] * parts,
        in_specs=[pl.BlockSpec(memory_space=pltpu.SMEM), vmem, vmem],
        out_specs=[vmem] * parts,
        compiler_params=pltpu.CompilerParams(vmem_limit_bytes=32 * 1024 * 1024),
        cost_estimate=pl.CostEstimate(
            flops=2 * 16 * weights.shape[0] * count * rows * cols,
            bytes_accessed=2 * frames.size + 4 * sums * rows * cols,
            transcendentals=0,
        ),
    )(place, weights, frames)


def choose_kernel(codes_ref, *refs):
    *sums_refs, out_ref = refs
    kinds, rows, cols = sums_refs[0].shape
    half = cols // 2
    params = kinds // CLASSES
    targets, planes, pair, _ = out_ref.shape
    shown = targets * pair // rows
    for plane in range(planes):
        first = plane // params * half
        level = codes_ref[:, first : first + half] & (CLASSES - 1)
        own = None
        for kind in range(CLASSES):
            at = (kind * params + plane % params, slice(None), slice(first, first + half))
            total = (sums_refs[0][at] + sums_refs[1][at]) + (sums_refs[2][at] + sums_refs[3][at])
            own = total if own is None else jnp.where(level == kind, total, own)
        for target in range(targets):
            begin = (target + FIRST_Z) % targets // shown * pair
            out_ref[target, plane] = own[begin : begin + pair]


def choose(codes, sums, targets, pair):
    kinds, _, cols = sums[0].shape
    vmem = pl.BlockSpec(memory_space=pltpu.VMEM)
    planes = 2 * (kinds // CLASSES)
    return pl.pallas_call(
        choose_kernel,
        out_shape=jax.ShapeDtypeStruct((targets, planes, pair, cols // 2), jnp.float32),
        in_specs=[vmem] * (1 + len(sums)),
        out_specs=vmem,
        compiler_params=pltpu.CompilerParams(vmem_limit_bytes=32 * 1024 * 1024),
    )(codes, *sums)


def exchange(block, count):
    order = [(FIRST_Z + i) % count for i in range(count)]
    return lax.all_to_all(block, "z", 0, 0, axis_index_groups=[order], tiled=True)


def shifted(block, axis, count, by):
    pairs = [(i, i + by) for i in range(count) if 0 <= i + by < count]
    return lax.ppermute(block, axis, pairs)


def tv_pass(field, fitted, row_first, col_first, rows_all, cols_all):
    rows = field.shape[1] - 1
    cols = field.shape[2] - 1
    here = field[:, :rows, :cols]
    row_ids = row_first + lax.broadcasted_iota(jnp.int32, (1, rows, cols), 1)
    col_ids = col_first + lax.broadcasted_iota(jnp.int32, (1, rows, cols), 2)
    grad_x = field[:, 1:, :cols] - here
    grad_y = field[:, :rows, 1:] - here
    grad_x = jnp.where((row_ids >= 0) & (row_ids <= rows_all - 2), grad_x, 0.0)
    grad_y = jnp.where((col_ids >= 0) & (col_ids <= cols_all - 2), grad_y, 0.0)
    length = jnp.sqrt(grad_x * grad_x + grad_y * grad_y + EPS_TV * EPS_TV)
    flux_x = grad_x / length
    flux_y = grad_y / length
    diverge = flux_x[:, 1:, 1:] - flux_x[:, :-1, 1:] + flux_y[:, 1:, 1:] - flux_y[:, 1:, :-1]
    inner = field[:, 1:rows, 1:cols]
    return inner + STEP_TV * (diverge - (inner - fitted))


def on_device(frames, freqs, valid, classes):
    frame_count = frames.shape[0]
    x_devs = lax.axis_size("x")
    z_devs = lax.axis_size("z")
    time_devs = x_devs * z_devs
    strip_devs = lax.axis_size("strip")
    total_frames = frame_count * time_devs
    tile_rows, tile_cols = valid.shape
    x_here = lax.axis_index("x")
    tm_here = lax.axis_index(TM)

    pair = 2 * tile_rows
    codes = classes + CLASSES * valid
    codes = exchange(jnp.broadcast_to(codes[None], (z_devs, *codes.shape)), z_devs)
    codes = jnp.concatenate([codes[z_devs - FIRST_Z :], codes[: z_devs - FIRST_Z]])
    codes = codes.reshape(-1, tile_cols)

    start, offset, rows = class_system(freqs, total_frames)
    times_here = tm_here * frame_count + jnp.arange(frame_count, dtype=jnp.int32)
    table_here = angle_table(freqs, times_here, total_frames).astype(jnp.float32)
    by_class = jnp.transpose(rows, (2, 0, 1)).reshape(CLASSES * 3, -1)
    weights = jnp.sum(by_class[:, :, None] * table_here[None], axis=1)
    place = jnp.full((1,), x_here, jnp.int32)
    sums = project(place, split_terms(weights), frames, x_devs)

    parts = [sums[0]]
    for shift in (1, 3, 2):
        pairs = [(i, (i + shift) % x_devs) for i in range(x_devs)]
        parts.append(lax.ppermute(sums[shift], "x", pairs))
    own = choose(codes, parts, z_devs, pair)
    own = jnp.sum(exchange(own, z_devs), axis=0)
    delta = jnp.concatenate([own[:3], own[3:]], axis=2)
    codes = lax.dynamic_slice_in_dim(codes, lax.axis_index("z") // 2 * pair, pair, 0)
    classes = codes % CLASSES
    here = start_params(classes)
    base = jnp.zeros_like(here)
    for level in range(CLASSES):
        base = jnp.where((classes == level)[None], offset[:, level][:, None, None], base)
    fitted = jnp.where((codes >= CLASSES)[None], here + (delta - base), here)

    wide = TV_PASSES
    left = shifted(fitted[:, :, tile_cols - wide :], "strip", strip_devs, 1)
    right = shifted(fitted[:, :, :wide], "strip", strip_devs, -1)
    band = jnp.concatenate([left, fitted, right], axis=2)
    above = shifted(band[:, pair - wide :], TM, time_devs, 2)
    below = shifted(band[:, :wide], TM, time_devs, -2)
    field = jnp.concatenate([above, band, below], axis=1)
    pair_first = lax.div(tm_here, 2) * pair
    row_first = pair_first - wide
    col_first = lax.axis_index("strip") * tile_cols - wide
    rows_all = tile_rows * time_devs
    cols_all = tile_cols * strip_devs
    fit = field
    for step in range(TV_PASSES):
        fit = fit[:, 1:-1, 1:-1]
        field = tv_pass(field, fit, row_first + step, col_first + step, rows_all, cols_all)
    return lax.dynamic_slice_in_dim(field, tm_here * tile_rows - pair_first, tile_rows, 1)


def solution(mesh):
    strip_devs = mesh.shape["strip"]
    x_devs = 4
    grid = Mesh(mesh.devices.reshape(x_devs, -1, strip_devs), ("x", "z", "strip"))
    placed = (P(TM, None, "strip"), P(), P(TM, "strip"), P(TM, "strip"))
    return jax.shard_map(
        on_device, mesh=grid, in_specs=placed, out_specs=P(None, TM, "strip"), check_vma=False
    )
```

```python
import math

import jax
import jax.numpy as jnp
import numpy as np
from jax import lax
from jax.experimental import pallas as pl
from jax.experimental.pallas import tpu as pltpu
from jax.sharding import Mesh, PartitionSpec as P

TV_PASSES = 3
EPS_TV = 1.0
STEP_TV = 0.2
CLASSES = 4
TM = ("x", "z")
FIRST_Z = 11


def angle_table(freqs, times, total):
    phase = freqs[:, None] * times[None, :] % total
    angle = phase.astype(jnp.float32) * (2.0 * math.pi / total)
    return jnp.concatenate([jnp.cos(angle), -jnp.sin(angle)], axis=0).astype(jnp.bfloat16)


def start_params(classes):
    level = classes.astype(jnp.float32)
    return jnp.stack([-0.3 + 0.2 * level, 0.5 - 0.3 * level, -0.5 + 0.25 * level])


def model_pieces(start, freqs):
    alpha_par, beta_par, gamma_par = (start[0], start[1], start[2])
    weight = jnp.sqrt(freqs.astype(jnp.float32) / 8.0)[:, None]
    amp = jnp.exp(alpha_par)
    tanh_b = jnp.tanh(beta_par)
    refl = 0.8 * tanh_b
    slope = 0.8 * (1.0 - tanh_b * tanh_b)
    depth = jnp.exp(gamma_par) * weight
    decay = jnp.exp(-2.0 * depth)
    e_re = decay * jnp.cos(2.0 * depth)
    e_im = -decay * jnp.sin(2.0 * depth)
    g_re = refl * e_re
    g_im = refl * e_im
    d_re = 1.0 - g_re
    d_im = -g_im
    denom = d_re * d_re + d_im * d_im
    q_re = ((1.0 + g_re) * d_re + g_im * d_im) / denom
    q_im = (g_im * d_re - (1.0 + g_re) * d_im) / denom
    scale = amp / (math.sqrt(2.0) * weight)

    def project(z_re, z_im):
        return jnp.concatenate([scale * (z_re + z_im), scale * (z_im - z_re)], axis=0)

    den_sq = denom * denom
    p_re = 2.0 * (d_re * d_re - d_im * d_im) / den_sq
    p_im = -4.0 * d_re * d_im / den_sq
    zb_re = (p_re * e_re - p_im * e_im) * slope
    zb_im = (p_re * e_im + p_im * e_re) * slope
    h_re = -2.0 * depth * (g_re - g_im)
    h_im = -2.0 * depth * (g_re + g_im)
    zc_re = p_re * h_re - p_im * h_im
    zc_im = p_re * h_im + p_im * h_re
    return jnp.stack([project(q_re, q_im), project(zb_re, zb_im), project(zc_re, zc_im)])


def class_system(freqs, total_frames):
    start = start_params(jnp.arange(CLASSES, dtype=jnp.int32))
    jac = model_pieces(start, freqs)
    mat = jnp.sum(jac[:, None] * jac[None, :], axis=2)
    damping = 0.1 * (mat[0, 0] + mat[1, 1] + mat[2, 2]) / 3.0 + 0.01
    a00 = mat[0, 0] + damping
    a11 = mat[1, 1] + damping
    a22 = mat[2, 2] + damping
    a01 = mat[0, 1]
    a02 = mat[0, 2]
    a12 = mat[1, 2]
    c00 = a11 * a22 - a12 * a12
    c01 = a02 * a12 - a01 * a22
    c02 = a01 * a12 - a02 * a11
    c11 = a00 * a22 - a02 * a02
    c12 = a01 * a02 - a00 * a12
    c22 = a00 * a11 - a01 * a01
    determinant = a00 * c00 + a01 * c01 + a02 * c02
    inverse = jnp.stack(
        [jnp.stack([c00, c01, c02]), jnp.stack([c01, c11, c12]), jnp.stack([c02, c12, c22])]
    ) / determinant
    model_rhs = mat[:, 0]
    offset = jnp.sum(inverse * model_rhs[None], axis=1)
    rows = jnp.sum(inverse[:, :, None, :] * jac[None], axis=1) / math.sqrt(total_frames)
    return start, offset, rows


def split_terms(value):
    terms = []
    for _ in range(3):
        term = lax.reduce_precision(value, 8, 7)
        terms.append(term.astype(jnp.bfloat16))
        value = value - term
    return jnp.concatenate(terms, axis=0)


def project_kernel(place_ref, weights_ref, frames_ref, *outs):
    group = 16
    count, _, cols = frames_ref.shape
    sums = weights_ref.shape[0]
    tall, wide = sums * group, count * group
    pick_row = lax.broadcasted_iota(jnp.int32, (tall, sums), 0) // group
    pick_col = lax.broadcasted_iota(jnp.int32, (tall, sums), 1)
    spread_rows = (pick_row == pick_col).astype(jnp.float32).astype(jnp.bfloat16)
    copy_row = lax.broadcasted_iota(jnp.int32, (count, wide), 0)
    copy_col = lax.broadcasted_iota(jnp.int32, (count, wide), 1) // group
    spread_cols = (copy_row == copy_col).astype(jnp.float32).astype(jnp.bfloat16)
    tall_by = jnp.dot(spread_rows, weights_ref[...], preferred_element_type=jnp.float32)
    full = jnp.dot(tall_by.astype(jnp.bfloat16), spread_cols, preferred_element_type=jnp.float32)
    same = (
        lax.broadcasted_iota(jnp.int32, (tall, wide), 0) % group
        == lax.broadcasted_iota(jnp.int32, (tall, wide), 1) % group
    )
    matrix = jnp.where(same, full, 0.0).astype(jnp.bfloat16)
    third = tall // 3
    parts = len(outs)
    for shift, out_ref in enumerate(outs):
        rows = out_ref.shape[1]
        first = lax.rem(place_ref[0] + shift, parts) * rows
        for step in range(rows // group):
            begin = pl.multiple_of(first + step * group, group)
            block = frames_ref[:, pl.ds(begin, group), :].reshape(wide, cols)
            got = jnp.dot(matrix, block, preferred_element_type=jnp.float32)
            total = (got[2 * third :] + got[third : 2 * third]) + got[:third]
            out_ref[:, step * group : (step + 1) * group, :] = total.reshape(sums // 3, group, cols)


def project(place, weights, frames, parts):
    count, rows, cols = frames.shape
    sums = weights.shape[0] // 3
    vmem = pl.BlockSpec(memory_space=pltpu.VMEM)
    out = jax.ShapeDtypeStruct((sums, rows // parts, cols), jnp.float32)
    return pl.pallas_call(
        project_kernel,
        out_shape=[out] * parts,
        in_specs=[pl.BlockSpec(memory_space=pltpu.SMEM), vmem, vmem],
        out_specs=[vmem] * parts,
        compiler_params=pltpu.CompilerParams(vmem_limit_bytes=32 * 1024 * 1024),
        cost_estimate=pl.CostEstimate(
            flops=2 * 16 * weights.shape[0] * count * rows * cols,
            bytes_accessed=2 * frames.size + 4 * sums * rows * cols,
            transcendentals=0,
        ),
    )(place, weights, frames)


def choose_kernel(codes_ref, *refs):
    *sums_refs, out_ref = refs
    kinds, rows, cols = sums_refs[0].shape
    half = cols // 2
    params = kinds // CLASSES
    targets, planes, pair, _ = out_ref.shape
    shown = targets * pair // rows
    for plane in range(planes):
        first = plane // params * half
        level = codes_ref[:, first : first + half] & (CLASSES - 1)
        own = None
        for kind in range(CLASSES):
            at = (kind * params + plane % params, slice(None), slice(first, first + half))
            total = (sums_refs[0][at] + sums_refs[1][at]) + (sums_refs[2][at] + sums_refs[3][at])
            own = total if own is None else jnp.where(level == kind, total, own)
        for target in range(targets):
            begin = (target + FIRST_Z) % targets // shown * pair
            out_ref[target, plane] = own[begin : begin + pair]


def choose(codes, sums, targets, pair):
    kinds, _, cols = sums[0].shape
    vmem = pl.BlockSpec(memory_space=pltpu.VMEM)
    planes = 2 * (kinds // CLASSES)
    return pl.pallas_call(
        choose_kernel,
        out_shape=jax.ShapeDtypeStruct((targets, planes, pair, cols // 2), jnp.float32),
        in_specs=[vmem] * (1 + len(sums)),
        out_specs=vmem,
        compiler_params=pltpu.CompilerParams(vmem_limit_bytes=32 * 1024 * 1024),
    )(codes, *sums)


def exchange(block, count):
    order = [(FIRST_Z + i) % count for i in range(count)]
    return lax.all_to_all(block, "z", 0, 0, axis_index_groups=[order], tiled=True)


def shifted(block, axis, count, by):
    pairs = [(i, (i + by) % count) for i in range(count)]
    return lax.ppermute(block, axis, pairs)


def tv_pass(field, fitted, row_first, col_first, rows_all, cols_all):
    rows = field.shape[1] - 1
    cols = field.shape[2] - 1
    here = field[:, :rows, :cols]
    row_ids = row_first + lax.broadcasted_iota(jnp.int32, (1, rows, cols), 1)
    col_ids = col_first + lax.broadcasted_iota(jnp.int32, (1, rows, cols), 2)
    grad_x = field[:, 1:, :cols] - here
    grad_y = field[:, :rows, 1:] - here
    grad_x = jnp.where((row_ids >= 0) & (row_ids <= rows_all - 2), grad_x, 0.0)
    grad_y = jnp.where((col_ids >= 0) & (col_ids <= cols_all - 2), grad_y, 0.0)
    length = jnp.sqrt(grad_x * grad_x + grad_y * grad_y + EPS_TV * EPS_TV)
    flux_x = grad_x / length
    flux_y = grad_y / length
    diverge = flux_x[:, 1:, 1:] - flux_x[:, :-1, 1:] + flux_y[:, 1:, 1:] - flux_y[:, 1:, :-1]
    inner = field[:, 1:rows, 1:cols]
    return inner + STEP_TV * (diverge - (inner - fitted))


def on_device(frames, freqs, valid, classes):
    frame_count = frames.shape[0]
    x_devs = lax.axis_size("x")
    z_devs = lax.axis_size("z")
    time_devs = x_devs * z_devs
    strip_devs = lax.axis_size("strip")
    total_frames = frame_count * time_devs
    tile_rows, tile_cols = valid.shape
    x_here = lax.axis_index("x")
    tm_here = lax.axis_index(TM)

    pair = 2 * tile_rows
    codes = classes + CLASSES * valid
    codes = exchange(jnp.broadcast_to(codes[None], (z_devs, *codes.shape)), z_devs)
    codes = jnp.concatenate([codes[z_devs - FIRST_Z :], codes[: z_devs - FIRST_Z]])
    codes = codes.reshape(-1, tile_cols)

    start, offset, rows = class_system(freqs, total_frames)
    times_here = tm_here * frame_count + jnp.arange(frame_count, dtype=jnp.int32)
    table_here = angle_table(freqs, times_here, total_frames).astype(jnp.float32)
    by_class = jnp.transpose(rows, (2, 0, 1)).reshape(CLASSES * 3, -1)
    weights = jnp.sum(by_class[:, :, None] * table_here[None], axis=1)
    place = jnp.full((1,), x_here, jnp.int32)
    sums = project(place, split_terms(weights), frames, x_devs)

    parts = [sums[0]]
    for shift in (1, 3, 2):
        pairs = [(i, (i + shift) % x_devs) for i in range(x_devs)]
        parts.append(lax.ppermute(sums[shift], "x", pairs))
    own = choose(codes, parts, z_devs, pair)
    own = jnp.sum(exchange(own, z_devs), axis=0)
    delta = jnp.concatenate([own[:3], own[3:]], axis=2)
    codes = lax.dynamic_slice_in_dim(codes, lax.axis_index("z") // 2 * pair, pair, 0)
    classes = codes % CLASSES
    here = start_params(classes)
    base = jnp.zeros_like(here)
    for level in range(CLASSES):
        base = jnp.where((classes == level)[None], offset[:, level][:, None, None], base)
    fitted = jnp.where((codes >= CLASSES)[None], here + (delta - base), here)

    wide = TV_PASSES
    left = shifted(fitted[:, :, tile_cols - wide :], "strip", strip_devs, 1)
    right = shifted(fitted[:, :, :wide], "strip", strip_devs, -1)
    band = jnp.concatenate([left, fitted, right], axis=2)
    above = shifted(band[:, pair - wide :], TM, time_devs, 2)
    below = shifted(band[:, :wide], TM, time_devs, -2)
    field = jnp.concatenate([above, band, below], axis=1)
    pair_first = lax.div(tm_here, 2) * pair
    row_first = pair_first - wide
    col_first = lax.axis_index("strip") * tile_cols - wide
    rows_all = tile_rows * time_devs
    cols_all = tile_cols * strip_devs
    fit = field
    for step in range(TV_PASSES):
        fit = fit[:, 1:-1, 1:-1]
        field = tv_pass(field, fit, row_first + step, col_first + step, rows_all, cols_all)
    return lax.dynamic_slice_in_dim(field, tm_here * tile_rows - pair_first, tile_rows, 1)


def solution(mesh):
    strip_devs = mesh.shape["strip"]
    x_devs = 4
    grid = Mesh(mesh.devices.reshape(x_devs, -1, strip_devs), ("x", "z", "strip"))
    placed = (P(TM, None, "strip"), P(), P(TM, "strip"), P(TM, "strip"))
    return jax.shard_map(
        on_device, mesh=grid, in_specs=placed, out_specs=P(None, TM, "strip"), check_vma=False
    )
```
